256 devices in a mesh: dp: 4 (over x), expert: 32 (over z, y), tensor: 2 (over core).
Axes of the slice: x: 4, y: 4, z: 8, core: 2. Of those that a mesh axis runs over, the one named last changes fastest.
Arguments:
- tokens: bfloat16 [8192, 2048], P(('dp', 'expert')), may hold values from -6 to 6
- expert_ids: int32 [8192, 8], P(('dp', 'expert')), may hold values from 0 to 63, all different within a row; in each aligned block of 64 rows (0 to 63, 64 to 127, ...) at most 12 rows name the same one
- route_weights: bfloat16 [8192, 8], P(('dp', 'expert')), may hold values from 0.049804688 to 0.34960938
- grad_out: bfloat16 [8192, 2048], P(('dp', 'expert')), may hold values from -6 to 6
- w_gate: bfloat16 [64, 2048, 768], P('expert', None, 'tensor'), may hold values from -0.125 to 0.125
- w_up: bfloat16 [64, 2048, 768], P('expert', None, 'tensor'), may hold values from -0.125 to 0.125
- w_down: bfloat16 [64, 768, 2048], P('expert', 'tensor'), may hold values from -0.21875 to 0.21875
Outputs:
- mixed: bfloat16 [8192, 2048], P(('dp', 'expert'))
- grad_x: bfloat16 [8192, 2048], P(('dp', 'expert'))
- grad_weights: float32 [8192, 8], P(('dp', 'expert'))
- grad_gate: bfloat16 [64, 2048, 768], P('expert', 'dp', 'tensor')
- grad_up: bfloat16 [64, 2048, 768], P('expert', 'dp', 'tensor')
- grad_down: bfloat16 [64, 768, 2048], P('expert', 'tensor', 'dp')
The draws below stay inside these ranges and needn't reach their ends.
Inputs may be any that keep to these rules, and one draw needn't show every extreme that they name: `expert_ids`: each row names 8 different experts; within each aligned block of 64 rows (the rows of one device) no expert is named more than 12 times, a bound that some block reaches.
All inputs are finite; a program needn't handle non-finite values.
Results may differ from the reference program's by a relative error of at most 0.0064.
Values may be sent and summed in bfloat16 or wider, within the bound.
No kernel may reach another device: no remote copies, remote signals or barrier semaphores. Data moves between devices by JAX's collectives and lax.ppermute only.
A program may use at most 128 MiB of HBM per device.

```python
import math
from functools import partial
import jax
import jax.numpy as jnp
import numpy as np
from jax import lax

D = 2048
FF = 768
EXPERTS = 64
TOP = 8
TOK_DEV = 64
CAP = 12
TOKENS = 8192
N_DP = 4
N_EXPERT = 32
N_TENSOR = 2


def levels(rng, dims, cuts, smallest, high):
    factor_of, own = 1.0, jax.random.fold_in(rng, 6)
    for axis_at, blocks in cuts:
        heights = jnp.exp(jax.random.uniform(jax.random.fold_in(own, axis_at), (blocks,), jnp.float32, smallest / len(cuts), high / len(cuts)))
        factor_of = factor_of * jnp.repeat(heights, dims[axis_at] // blocks).reshape([-1 if axis == axis_at else 1 for axis in range(len(dims))])
    return factor_of


def deal_out(stream_key, own, number, rows, amount, top, limit, slope):
    sequence = jax.random.permutation(stream_key, amount)
    crowded, ordinary = portions_of(amount, rows * top, limit, slope, True), portions_of(amount, rows * top, limit, slope, False)
    places = jnp.arange(amount)

    def named(lengths, offset_by):
        used = int((lengths > 0).sum())
        fixed = max(1, used // 4)
        passed = fixed + (places - fixed + offset_by * (used - fixed)) % max(1, amount - fixed)
        return jnp.zeros((amount,), jnp.int32).at[sequence[jnp.where(places < fixed, places, passed)]].set(jnp.asarray(lengths, jnp.int32))

    lengths = jnp.where(number % 4 == 0, named(crowded, number // 4), named(ordinary, number - number // 4 - 1))
    mixed = jax.random.permutation(jax.random.fold_in(own, 3), amount)
    giver, taker = mixed[0:amount // 2 * 2:2], mixed[1:amount // 2 * 2:2]
    slack = jnp.minimum(lengths[giver] - 1, limit - lengths[taker]) // 2
    slack = jnp.where((giver == sequence[0]) | (taker == sequence[0]) | (lengths[taker] == 0), 0, jnp.maximum(slack, 0))
    passed = jax.random.randint(jax.random.fold_in(own, 4), (amount // 2,), 0, 1 << 20) % (slack + 1)
    lengths = lengths.at[giver].add(-passed).at[taker].add(passed)
    members = jnp.searchsorted(jnp.cumsum(lengths), jnp.arange(rows * top), side="right").astype(jnp.int32)
    listing = members.reshape(top, rows).T
    listing = listing[jax.random.permutation(jax.random.fold_in(own, 1), rows)]
    offset_by = jax.random.randint(jax.random.fold_in(own, 2), (rows, 1), 0, top)
    return jnp.take_along_axis(listing, (jnp.arange(top)[None, :] + offset_by) % top, axis=1)


def portions_of(amount, total, most, lean, full):
    weights = [(1 << 20) // math.isqrt(grade ** lean) + 1 for grade in range(1, amount + 1)]
    largest = most if full else min(most, max(-(-total // amount), total * weights[0] // sum(weights)))
    least = 1 if total - largest >= amount - 1 else 0
    counts, spare = [largest] + [least] * (amount - 1), total - largest - least * (amount - 1)
    while spare > 0:
        movable = [i for i in range(1, amount) if counts[i] < largest] or [i for i in range(1, amount) if counts[i] < most]
        mass, remaining = sum([weights[i] for i in movable]), spare
        for i in movable:
            addition = min(most - counts[i], max(1, remaining * weights[i] // mass), spare)
            counts[i] = counts[i] + addition
            spare = spare - addition
    return np.array(counts)


def gaussian(rng, shape, deviation, most, pieces=(), kind=jnp.bfloat16):
    array = deviation * jax.random.normal(rng, shape, jnp.float32)
    if pieces:
        array = array * levels(rng, shape, pieces, -0.22, 0.18)
    return jnp.clip(array, -most, most).astype(kind)


def setup_inputs(seed: int = 0) -> dict:
    key_of = jax.random.split(jax.random.key(seed), 8)
    tokens = gaussian(key_of[0], (TOKENS, D), 1.0, 6.0, ((0, 128),))
    expert_ids_keys = jax.random.split(jax.random.fold_in(key_of[1], 1), TOKENS // TOK_DEV)
    expert_ids_turns = jax.random.permutation(jax.random.fold_in(key_of[1], 3), TOKENS // TOK_DEV)
    expert_ids = jax.vmap(lambda own, number: deal_out(jax.random.fold_in(key_of[1], 2), own, number, TOK_DEV, EXPERTS, TOP, CAP, 2))(expert_ids_keys, expert_ids_turns).reshape((TOKENS, TOP))
    route_weights = jnp.clip(0.049804688 + 0.2998047 * jax.random.uniform(key_of[2], (TOKENS, TOP), jnp.float32) ** levels(key_of[2], (TOKENS, TOP), ((0, 128),), -0.2, 0.2), 0.049804688, 0.34960938).astype(jnp.bfloat16)
    grad_out = gaussian(key_of[3], (TOKENS, D), 1.0, 6.0, ((0, 128),))
    w_gate = gaussian(key_of[4], (EXPERTS, D, FF), D ** -0.5, 0.125, ((0, 32), (2, 2)))
    w_up = gaussian(key_of[5], (EXPERTS, D, FF), D ** -0.5, 0.125, ((0, 32), (2, 2)))
    w_down = gaussian(key_of[6], (EXPERTS, FF, D), FF ** -0.5, 0.21875, ((0, 32), (1, 2)))
    return dict(tokens=tokens, expert_ids=expert_ids, route_weights=route_weights, grad_out=grad_out, w_gate=w_gate, w_up=w_up, w_down=w_down)


def route_tables(expert_ids, route_weights, experts, capacity):
    tok_count, top_count = expert_ids.shape
    labels = jnp.arange(experts, dtype=jnp.int32)
    onehot = (expert_ids[:, :, None] == labels[None, None, :]).astype(jnp.int32)
    flattened = onehot.reshape(tok_count * top_count, experts)
    earlier = jnp.cumsum(flattened, axis=0) - flattened
    slot_index = jnp.sum(earlier * flattened, axis=1).reshape(tok_count, top_count)
    target_slot = expert_ids * capacity + slot_index
    positions = jnp.arange(experts * capacity, dtype=jnp.int32)
    placed = target_slot[:, :, None] == positions[None, None, :]
    picked = jnp.any(placed, axis=1).astype(jnp.bfloat16)
    carried = jnp.sum(jnp.where(placed, route_weights.astype(jnp.float32)[:, :, None], jnp.float32(0.0)), axis=1).astype(jnp.bfloat16)
    return placed, picked, carried


def expert_pass(operands):
    rows_x, rows_g, gate_w, up_w, down_w = operands
    gate_pre = jnp.dot(rows_x, gate_w, preferred_element_type=jnp.float32)
    up_pre = jnp.dot(rows_x, up_w, preferred_element_type=jnp.float32)
    sigmoid_gate = jax.nn.sigmoid(gate_pre)
    activated = gate_pre * sigmoid_gate
    hidden = (activated * up_pre).astype(jnp.bfloat16)
    grad_hidden = jnp.dot(rows_g, down_w.T, preferred_element_type=jnp.float32)
    grad_gate_pre = (grad_hidden * up_pre * sigmoid_gate * (1.0 + gate_pre * (1.0 - sigmoid_gate))).astype(jnp.bfloat16)
    grad_up_pre = (grad_hidden * activated).astype(jnp.bfloat16)
    half_width = FF // N_TENSOR
    out_total = jnp.zeros((rows_x.shape[0], D), jnp.float32)
    dx_total = jnp.zeros((rows_x.shape[0], D), jnp.float32)
    for member in range(N_TENSOR):
        lower = member * half_width
        upper = lower + half_width
        out_piece = jnp.dot(hidden[:, lower:upper], down_w[lower:upper], preferred_element_type=jnp.float32)
        out_total = out_total + lax.optimization_barrier(out_piece.astype(jnp.bfloat16)).astype(jnp.float32)
        dx_piece = jnp.dot(grad_gate_pre[:, lower:upper], gate_w[:, lower:upper].T, preferred_element_type=jnp.float32)
        dx_piece = dx_piece + jnp.dot(grad_up_pre[:, lower:upper], up_w[:, lower:upper].T, preferred_element_type=jnp.float32)
        dx_total = dx_total + lax.optimization_barrier(dx_piece.astype(jnp.bfloat16)).astype(jnp.float32)
    grad_gate_w = jnp.dot(rows_x.T, grad_gate_pre, preferred_element_type=jnp.float32).astype(jnp.bfloat16)
    grad_up_w = jnp.dot(rows_x.T, grad_up_pre, preferred_element_type=jnp.float32).astype(jnp.bfloat16)
    grad_down_w = jnp.dot(hidden.T, rows_g, preferred_element_type=jnp.float32).astype(jnp.bfloat16)
    return out_total, dx_total, grad_gate_w, grad_up_w, grad_down_w


def send_block(operands):
    picked_block, carried_block, token_block, grad_block = operands
    rows_sent = jnp.dot(picked_block.T, token_block, preferred_element_type=jnp.float32).astype(jnp.bfloat16)
    grads_sent = jnp.dot(carried_block.T, grad_block, preferred_element_type=jnp.float32).astype(jnp.bfloat16)
    return rows_sent, grads_sent


def combine_block(operands):
    placed_block, picked_block, carried_block, grad_block, out_block, dx_block = operands
    mixed_block = jnp.dot(carried_block.astype(jnp.float32), out_block, precision=lax.Precision.HIGHEST)
    grad_x_block = jnp.dot(picked_block.astype(jnp.float32), dx_block, precision=lax.Precision.HIGHEST)
    scores = jnp.dot(grad_block.astype(jnp.float32), out_block.T, precision=lax.Precision.HIGHEST)
    weight_block = jnp.sum(jnp.where(placed_block, scores[:, None, :], jnp.float32(0.0)), axis=2)
    return mixed_block.astype(jnp.bfloat16), grad_x_block.astype(jnp.bfloat16), weight_block


def reference(tokens, expert_ids, route_weights, grad_out, w_gate, w_up, w_down):
    blocks = N_DP * N_EXPERT
    slot_count = EXPERTS * CAP
    token_blocks = tokens.reshape(blocks, TOK_DEV, D)
    grad_blocks = grad_out.reshape(blocks, TOK_DEV, D)
    id_blocks = expert_ids.reshape(blocks, TOK_DEV, TOP)
    weight_blocks = route_weights.reshape(blocks, TOK_DEV, TOP)
    tables = partial(route_tables, experts=EXPERTS, capacity=CAP)
    placed, picked, carried = jax.vmap(tables)(id_blocks, weight_blocks)
    sent_rows, sent_grads = lax.map(send_block, (picked, carried, token_blocks, grad_blocks))
    expert_rows = sent_rows.reshape(blocks, EXPERTS, CAP, D).transpose(1, 0, 2, 3).reshape(EXPERTS, blocks * CAP, D)
    expert_grads = sent_grads.reshape(blocks, EXPERTS, CAP, D).transpose(1, 0, 2, 3).reshape(EXPERTS, blocks * CAP, D)
    out_total, dx_total, grad_gate, grad_up, grad_down = lax.map(expert_pass, (expert_rows, expert_grads, w_gate, w_up, w_down))
    back_out = out_total.reshape(EXPERTS, blocks, CAP, D).transpose(1, 0, 2, 3).reshape(blocks, slot_count, D)
    back_dx = dx_total.reshape(EXPERTS, blocks, CAP, D).transpose(1, 0, 2, 3).reshape(blocks, slot_count, D)
    mixed, grad_x, grad_weights = lax.map(combine_block, (placed, picked, carried, grad_blocks, back_out, back_dx))
    mixed = mixed.reshape(blocks * TOK_DEV, D)
    grad_x = grad_x.reshape(blocks * TOK_DEV, D)
    grad_weights = grad_weights.reshape(blocks * TOK_DEV, TOP)
    return mixed, grad_x, grad_weights, grad_gate, grad_up, grad_down
```

```python
import functools

import jax
import jax.numpy as jnp
from jax import lax
from jax.experimental import pallas as pl
from jax.experimental.pallas import tpu as pltpu
from jax.sharding import PartitionSpec as P

CAP = 12
NZ, NY, NDP = 8, 4, 4
TOK = 64
ALL = NZ * TOK
BLK = NZ * CAP
ROWS = NY * BLK
HALF = 1024
AUX = 128
WIDE = HALF + AUX
SLICE = 512
BF, F32 = jnp.bfloat16, jnp.float32
VMEM_LIMIT = 48 * 1024 * 1024

Z_PERM = {k: [(z * NY + y, (z + k) % NZ * NY + y) for z in range(NZ) for y in range(NY)] for k in (1, -1)}
Y_PERM = {k: [(z * NY + y, z * NY + (y + k) % NY) for z in range(NZ) for y in range(NY)] for k in (1, 2, 3)}
D_PERM = {k: [(i, (i + k) % NDP) for i in range(NDP)] for k in (1, 2, 3)}
T_PERM = [(0, 1), (1, 0)]


def z_shift(v, k):
    return lax.ppermute(v, "expert", Z_PERM[k])


def y_shift(v, k):
    return lax.ppermute(v, "expert", Y_PERM[k])


def d_shift(v, k):
    return lax.ppermute(v, "dp", D_PERM[k % NDP])


def swap(v):
    return lax.ppermute(v, "tensor", T_PERM)


def call(kernel, outs, ins, scratch=(), grid=None, in_specs=None, out_specs=None, flops=0):
    moved = sum(v.size * v.dtype.itemsize for v in ins) + sum(o.size * o.dtype.itemsize for o in outs)
    extra = {} if grid is None else {"grid": grid}
    vm = pl.BlockSpec(memory_space=pltpu.VMEM)
    return pl.pallas_call(
        kernel,
        out_shape=outs,
        in_specs=in_specs or [vm] * len(ins),
        out_specs=out_specs or [vm] * len(outs),
        scratch_shapes=list(scratch),
        compiler_params=pltpu.CompilerParams(vmem_limit_bytes=VMEM_LIMIT),
        cost_estimate=pl.CostEstimate(flops=flops, bytes_accessed=moved, transcendentals=0),
        **extra,
    )(*ins)


def shape(*dims, dtype=BF):
    return jax.ShapeDtypeStruct(dims, dtype)


SMEM = pl.BlockSpec(memory_space=pltpu.SMEM)
VM = pl.BlockSpec(memory_space=pltpu.VMEM)


def place(pieces, into, cols):
    row = 0
    for ref in pieces:
        n = ref.shape[0]
        into[row : row + n, :] = ref[:, cols].astype(into.dtype)
        row += n


def one_hot(tab, oh, weighted):
    slot = lax.broadcasted_iota(jnp.int32, (BLK, ALL), 0).astype(F32)
    for e in range(2 * NY):
        value = tab[8 + e : 9 + e, :] if weighted else 1.0
        oh[e * BLK : (e + 1) * BLK, :] = jnp.where(tab[e : e + 1, :] == slot, value, 0.0).astype(BF)


def pick(oh, full, outs):
    for k, out in enumerate(outs):
        rows = jnp.dot(oh[k * 2 * BLK : (k + 1) * 2 * BLK, :], full[...], preferred_element_type=F32).astype(BF)
        out[0] = rows[:BLK]
        out[1] = rows[BLK:]


def pick_tokens_kernel(experts, *refs):
    pieces, (o0, o1, o2, o3, tab), (full, aux, hits, oh) = refs[:9], refs[9:14], refs[14:]
    place(pieces, full, slice(0, HALF))
    place(pieces, aux, slice(HALF, WIDE))
    turned = aux[...].T
    ids = turned[0:8, :].astype(jnp.int32)
    weights = turned[8:16, :]
    tab[16:24, :] = turned[0:8, :]
    hits[...] = jnp.zeros_like(hits)
    for e in range(2 * NY):
        same = ids == experts[e]
        hits[e : e + 1, :] = jnp.sum(jnp.where(same, 1.0, 0.0), axis=0, keepdims=True)
        tab[8 + e : 9 + e, :] = jnp.sum(jnp.where(same, weights, 0.0), axis=0, keepdims=True)
    before = lax.broadcasted_iota(jnp.int32, (ALL, ALL), 0)
    after = lax.broadcasted_iota(jnp.int32, (ALL, ALL), 1)
    earlier = jnp.where((before < after) & (before // TOK == after // TOK), 1.0, 0.0).astype(BF)
    rank = jnp.dot(hits[...].astype(BF), earlier, preferred_element_type=F32)
    block = (lax.broadcasted_iota(jnp.int32, (8, ALL), 1) // TOK).astype(F32)
    tab[0:8, :] = jnp.where(hits[0:8, :] > 0.0, block * CAP + rank[0:8, :], -1.0)
    one_hot(tab, oh, False)
    pick(oh, full, (o0, o1, o2, o3))


def pick_grads_kernel(tab, *refs):
    pieces, outs, full, (oh,) = refs[:9], refs[9:13], refs[13], refs[14:]
    place(pieces, full, slice(0, HALF))
    one_hot(tab, oh, True)
    pick(oh, full, outs)


def gather_rows(own, other, rows, core):
    for k in range(NY):
        span = slice(k * BLK, (k + 1) * BLK)
        rows[span, pl.ds(pl.multiple_of(core * HALF, HALF), HALF)] = own[k][0]
        rows[span, pl.ds(pl.multiple_of((1 - core) * HALF, HALF), HALF)] = other[k][0]


def cut_slices(info, rows, outs):
    outs[0][0] = rows[:, pl.ds(pl.multiple_of(info[1] * SLICE, SLICE), SLICE)]
    for k in range(1, NDP):
        at = info[1 + k] * SLICE + info[0] * (SLICE // 2)
        outs[k][0] = rows[:, pl.ds(pl.multiple_of(at, SLICE // 2), SLICE // 2)]


def forward_kernel(info, *refs):
    own, other, (w_gate, w_up, w_down) = refs[:4], refs[4:8], refs[8:11]
    slices, (act, slope, hidden, send), rows = refs[11:15], refs[15:19], refs[19]
    core = info[0]
    gather_rows(own, other, rows, core)
    cut_slices(info, rows, slices)
    gate = jnp.dot(rows[...], w_gate[0], preferred_element_type=F32)
    up = jnp.dot(rows[...], w_up[0], preferred_element_type=F32)
    sig = jax.nn.sigmoid(gate)
    activated = gate * sig
    act[0] = activated
    slope[0] = up * sig * (1.0 + gate * (1.0 - sig))
    hid = (activated * up).astype(BF)
    hidden[0] = hid
    far = w_down[0, :, pl.ds(pl.multiple_of((1 - core) * HALF, HALF), HALF)]
    send[0] = jnp.dot(hid, far, preferred_element_type=F32).astype(BF)


def out_kernel(info, hidden, w_down, got, *outs):
    near = w_down[0, :, pl.ds(pl.multiple_of(info[0] * HALF, HALF), HALF)]
    total = jnp.dot(hidden[0], near, preferred_element_type=F32) + got[0].astype(F32)
    for k in range(NY):
        outs[k][0] = total[k * BLK : (k + 1) * BLK].astype(BF)


NT = (((1,), (1,)), ((), ()))
TN = (((0,), (0,)), ((), ()))


def backward_kernel(info, *refs):
    own, other, (w_gate, w_up, w_down, act, slope) = refs[:4], refs[4:8], refs[8:13]
    slices, (gg, send), rows = refs[13:17], refs[17:19], refs[19]
    core = info[0]
    gather_rows(own, other, rows, core)
    cut_slices(info, rows, slices)
    grad = lax.dot_general(rows[...], w_down[0], NT, preferred_element_type=F32)
    d_gate = (grad * slope[0]).astype(BF)
    d_up = (grad * act[0]).astype(BF)
    gg[0, :, 0:384] = d_gate
    gg[0, :, 384:768] = d_up
    far = pl.ds(pl.multiple_of((1 - core) * HALF, HALF), HALF)
    total = lax.dot_general(d_gate, w_gate[0, far, :], NT, preferred_element_type=F32)
    total = total + lax.dot_general(d_up, w_up[0, far, :], NT, preferred_element_type=F32)
    send[0] = total.astype(BF)


def dx_kernel(info, gg, w_gate, w_up, got, *outs):
    near = pl.ds(pl.multiple_of(info[0] * HALF, HALF), HALF)
    total = lax.dot_general(gg[0, :, 0:384], w_gate[0, near, :], NT, preferred_element_type=F32)
    total = total + lax.dot_general(gg[0, :, 384:768], w_up[0, near, :], NT, preferred_element_type=F32)
    total = total + got[0].astype(F32)
    for k in range(NY):
        outs[k][0] = total[k * BLK : (k + 1) * BLK].astype(BF)


def lay_rows(pieces, rows):
    for k, ref in enumerate(pieces):
        for j in range(2):
            rows[(2 * k + j) * BLK : (2 * k + j + 1) * BLK, :] = ref[j]


def spread(total, outs, cols):
    near, (top, low), far = outs[:4], outs[4:6], outs[6:]
    for d in range(4):
        near[d][:, cols] = total[d * TOK : (d + 1) * TOK]
    top[:, cols] = total[4 * TOK : 4 * TOK + TOK // 2].astype(BF)
    low[:, cols] = total[4 * TOK + TOK // 2 : 5 * TOK].astype(BF)
    for d in range(3):
        far[d][:, cols] = total[(5 + d) * TOK : (6 + d) * TOK]


def mix_kernel(experts, tab, grads, *refs):
    pieces, outs, (rows, oh, turned) = refs[:4], refs[4:13], refs[13:]
    lay_rows(pieces, rows)
    one_hot(tab, oh, True)
    total = lax.dot_general(oh[...], rows[...], TN, preferred_element_type=F32)
    spread(total, outs, slice(0, HALF))
    scores = lax.dot_general(rows[...], grads[...], NT, preferred_element_type=F32)
    slot = lax.broadcasted_iota(jnp.int32, (BLK, ALL), 0).astype(F32)
    ids = tab[16:24, :].astype(jnp.int32)
    found = jnp.zeros((8, ALL), F32)
    for e in range(2 * NY):
        mine = jnp.where(tab[e : e + 1, :] == slot, scores[e * BLK : (e + 1) * BLK, :], 0.0)
        mine = jnp.sum(mine, axis=0, keepdims=True)
        found = found + jnp.where(ids == experts[e], mine, 0.0)
    high = found.astype(BF).astype(F32)
    turned[...] = jnp.zeros_like(turned)
    turned[0:8, :] = high
    turned[8:16, :] = found - high
    spread(turned[...].T, outs, slice(HALF, WIDE))


def unpick_kernel(tab, *refs):
    pieces, outs, (rows, oh) = refs[:4], refs[4:13], refs[13:]
    lay_rows(pieces, rows)
    one_hot(tab, oh, False)
    total = lax.dot_general(oh[...], rows[...], TN, preferred_element_type=F32)
    spread(total, outs, slice(0, HALF))


def gate_up_kernel(info, *refs):
    (own, n1, n2, n3, f1, f2, f3), (g0, g1, g2a, g2b, g3) = refs[:7], refs[7:12]
    d_gate, d_up, x_all, g_all = refs[12:]
    join(info, (own, n1, n2, n3, f1, f2, f3), x_all)
    stack((g0, g1, g2a, g2b, g3), g_all)
    total = lax.dot_general(x_all[...], g_all[...], TN, preferred_element_type=F32)
    d_gate[0] = total[:, 0:384].astype(BF)
    d_up[0] = total[:, 384:768].astype(BF)


def down_kernel(info, *refs):
    d_down, g_all, h_all = refs[12:]
    join(info, refs[:7], g_all)
    stack(refs[7:12], h_all)
    d_down[0] = lax.dot_general(h_all[...], g_all[...], TN, preferred_element_type=F32).astype(BF)


def join(info, parts, into):
    own, near, far = parts[0], parts[1:4], parts[4:7]
    half = SLICE // 2
    into[0:ROWS, :] = own[0]
    for k in range(1, NDP):
        span = slice(k * ROWS, (k + 1) * ROWS)
        into[span, pl.ds(pl.multiple_of(info[0] * half, half), half)] = near[k - 1][0]
        into[span, pl.ds(pl.multiple_of((1 - info[0]) * half, half), half)] = far[k - 1][0]


def stack(parts, into):
    v0, v1, v2a, v2b, v3 = parts
    into[0:ROWS, :] = v0[0]
    into[ROWS : 2 * ROWS, :] = v1[0]
    into[3 * ROWS : 4 * ROWS, :] = v3[0]

    @pl.when(pl.program_id(0) == 0)
    def _():
        into[2 * ROWS : 3 * ROWS, :] = v2a[...]

    @pl.when(pl.program_id(0) == 1)
    def _():
        into[2 * ROWS : 3 * ROWS, :] = v2b[...]


def z_gather(v):
    h = TOK // 2
    r1, l1 = z_shift(v, 1), z_shift(v, -1)
    r2, l2 = z_shift(r1, 1), z_shift(l1, -1)
    r3, l3 = z_shift(r2, 1), z_shift(l2, -1)
    r4, l4 = z_shift(r3[:h], 1), z_shift(l3[h:], -1)
    return [v, r1, r2, r3, r4, l4, l3, l2, l1]


def z_reduce(p0, p1, p2, p3, top, low, p5, p6, p7):
    h = TOK // 2
    r, l = z_shift(top, 1).astype(F32), z_shift(low, -1).astype(F32)
    r = p5 + jnp.pad(r, ((0, h), (0, 0)))
    l = p3 + jnp.pad(l, ((h, 0), (0, 0)))
    for a, b in ((p6, p2), (p7, p1)):
        r = a + z_shift(r.astype(BF), 1).astype(F32)
        l = b + z_shift(l.astype(BF), -1).astype(F32)
    return p0 + z_shift(r.astype(BF), 1).astype(F32) + z_shift(l.astype(BF), -1).astype(F32)


def dp_gather(v):
    right, left = d_shift(v, 1), d_shift(v, -1)
    return [v, right, d_shift(right[0], 1), d_shift(left[1], -1), left]


def dp_slices(slices):
    near = [d_shift(slices[k], k) for k in (1, 2, 3)]
    return [slices[0]] + near + [swap(v) for v in near]


def of_expert(*dims):
    return pl.BlockSpec((1,) + dims, lambda e: (e,) + (0,) * len(dims))


def whole(*dims):
    return pl.BlockSpec(dims, lambda e: (0,) * len(dims))


def per_device(tokens, expert_ids, route_weights, grad_out, w_gate, w_up, w_down):
    core = lax.axis_index("tensor")
    at = lax.axis_index("expert")
    z, y = at // NY, at % NY
    dp = lax.axis_index("dp")
    owners = (y + jnp.arange(2 * NY, dtype=jnp.int32) // 2) % NY
    experts = z * 2 * NY + owners * 2 + jnp.arange(2 * NY, dtype=jnp.int32) % 2
    info = jnp.concatenate([core[None], (dp + jnp.arange(NDP, dtype=jnp.int32)) % NDP]).astype(jnp.int32)

    x_half = lax.dynamic_slice_in_dim(tokens, core * HALF, HALF, axis=1)
    g_half = lax.dynamic_slice_in_dim(grad_out, core * HALF, HALF, axis=1)
    aux = jnp.concatenate([expert_ids.astype(BF), route_weights, jnp.zeros((TOK, AUX - 16), BF)], axis=1)
    x_pieces = z_gather(jnp.concatenate([x_half, aux], axis=1))
    g_pieces = z_gather(g_half)

    ring = [shape(2, BLK, HALF)] * NY
    *x_rows, tab = call(
        pick_tokens_kernel,
        ring + [shape(24, ALL, dtype=F32)],
        [experts] + x_pieces,
        [pltpu.VMEM((ALL, HALF), BF), pltpu.VMEM((ALL, AUX), F32), pltpu.VMEM((16, ALL), F32), pltpu.VMEM((2 * ROWS, ALL), BF)],
        in_specs=[SMEM] + [VM] * 9,
        flops=2 * 768 * 512 * 1024,
    )
    *g_rows, grads = call(
        pick_grads_kernel,
        ring + [shape(ALL, HALF)],
        [tab] + g_pieces,
        [pltpu.VMEM((2 * ROWS, ALL), BF)],
        flops=2 * 768 * 512 * 1024,
    )
    x_own = [x_rows[0]] + [y_shift(x_rows[k], k) for k in (1, 2, 3)]
    x_far = [swap(v) for v in x_own]
    g_own = [g_rows[0]] + [y_shift(g_rows[k], k) for k in (1, 2, 3)]
    g_far = [swap(v) for v in g_own]

    slices = [shape(2, ROWS, SLICE)] + [shape(2, ROWS, SLICE // 2)] * 3
    slice_specs = [of_expert(ROWS, SLICE)] + [of_expert(ROWS, SLICE // 2)] * 3
    block = [of_expert(BLK, HALF)] * 4
    wg_spec, wd_spec = of_expert(2048, 384), of_expert(384, 2048)
    sq = of_expert(ROWS, 384)
    *x_slices, act, slope, hidden, out_send = call(
        forward_kernel,
        slices + [shape(2, ROWS, 384, dtype=F32)] * 2 + [shape(2, ROWS, 384), shape(2, ROWS, HALF)],
        [info] + x_own + x_far + [w_gate, w_up, w_down],
        [pltpu.VMEM((ROWS, 2048), BF)],
        grid=(2,),
        in_specs=[SMEM] + block * 2 + [wg_spec, wg_spec, wd_spec],
        out_specs=slice_specs + [sq, sq, sq, of_expert(ROWS, HALF)],
        flops=2 * 768 * 2048 * 384 * 5 // 2,
    )
    out_rows = call(
        out_kernel,
        ring,
        [info, hidden, w_down, swap(out_send)],
        grid=(2,),
        in_specs=[SMEM, sq, wd_spec, of_expert(ROWS, HALF)],
        out_specs=block,
        flops=2 * 768 * 2048 * 384 // 2,
    )
    *g_slices, gg, dx_send = call(
        backward_kernel,
        slices + [shape(2, ROWS, 768), shape(2, ROWS, HALF)],
        [info] + g_own + g_far + [w_gate, w_up, w_down, act, slope],
        [pltpu.VMEM((ROWS, 2048), BF)],
        grid=(2,),
        in_specs=[SMEM] + block * 2 + [wg_spec, wg_spec, wd_spec, sq, sq],
        out_specs=slice_specs + [of_expert(ROWS, 768), of_expert(ROWS, HALF)],
        flops=2 * 768 * 2048 * 384 * 2,
    )
    dx_rows = call(
        dx_kernel,
        ring,
        [info, gg, w_gate, w_up, swap(dx_send)],
        grid=(2,),
        in_specs=[SMEM, of_expert(ROWS, 768), wg_spec, wg_spec, of_expert(ROWS, HALF)],
        out_specs=block,
        flops=2 * 768 * 2048 * 384,
    )

    def parts(width):
        full, split = shape(TOK, width, dtype=F32), shape(TOK // 2, width)
        return [full] * 4 + [split] * 2 + [full] * 3

    out_back = [out_rows[0]] + [y_shift(out_rows[k], NY - k) for k in (1, 2, 3)]
    mixed_parts = call(
        mix_kernel,
        parts(WIDE),
        [experts, tab, grads] + out_back,
        [pltpu.VMEM((2 * ROWS, HALF), BF), pltpu.VMEM((2 * ROWS, ALL), BF), pltpu.VMEM((AUX, ALL), F32)],
        in_specs=[SMEM] + [VM] * 6,
        flops=4 * 768 * 512 * 1024,
    )
    mixed_half = z_reduce(*mixed_parts)
    dx_back = [dx_rows[0]] + [y_shift(dx_rows[k], NY - k) for k in (1, 2, 3)]
    dx_parts = call(
        unpick_kernel,
        parts(HALF),
        [tab] + dx_back,
        [pltpu.VMEM((2 * ROWS, HALF), BF), pltpu.VMEM((2 * ROWS, ALL), BF)],
        flops=2 * 768 * 512 * 1024,
    )
    dx_half = z_reduce(*dx_parts).astype(BF)

    def both(half):
        other = swap(half)
        low, high = jnp.where(core == 0, half, other), jnp.where(core == 0, other, half)
        return jnp.concatenate([low, high], axis=1)

    mixed = both(mixed_half[:, :HALF].astype(BF))
    weight_half = mixed_half[:, HALF : HALF + 8] + mixed_half[:, HALF + 8 : HALF + 16]
    grad_weights = weight_half + swap(weight_half)
    grad_x = both(dx_half)

    slice_in = [of_expert(ROWS, SLICE)] + [of_expert(ROWS, SLICE // 2)] * 6
    (grad_down,) = call(
        down_kernel,
        [shape(2, 384, SLICE)],
        [info] + dp_slices(g_slices) + dp_gather(hidden),
        [pltpu.VMEM((NDP * ROWS, SLICE), BF), pltpu.VMEM((NDP * ROWS, 384), BF)],
        grid=(2,),
        in_specs=[SMEM] + slice_in + [sq, sq, whole(ROWS, 384), whole(ROWS, 384), sq],
        out_specs=[of_expert(384, SLICE)],
        flops=2 * 768 * 2048 * 384,
    )
    gg_spec = of_expert(ROWS, 768)
    grad_gate, grad_up = call(
        gate_up_kernel,
        [shape(2, SLICE, 384)] * 2,
        [info] + dp_slices(x_slices) + dp_gather(gg),
        [pltpu.VMEM((NDP * ROWS, SLICE), BF), pltpu.VMEM((NDP * ROWS, 768), BF)],
        grid=(2,),
        in_specs=[SMEM] + slice_in + [gg_spec, gg_spec, whole(ROWS, 768), whole(ROWS, 768), gg_spec],
        out_specs=[of_expert(SLICE, 384)] * 2,
        flops=2 * 768 * 2048 * 384 * 2,
    )
    return mixed, grad_x, grad_weights, grad_gate, grad_up, grad_down


def solution(mesh):
    tok = P(("dp", "expert"), None)
    return jax.shard_map(
        per_device,
        mesh=mesh,
        in_specs=(tok, tok, tok, tok, P("expert", None, "tensor"), P("expert", None, "tensor"), P("expert", "tensor", None)),
        out_specs=(tok, tok, tok, P("expert", "dp", "tensor"), P("expert", "dp", "tensor"), P("expert", "tensor", "dp")),
        check_vma=False,
    )
```

```python
import jax
import jax.numpy as jnp
from jax import lax
from jax.experimental import pallas as pl
from jax.experimental.pallas import tpu as pltpu
from jax.sharding import PartitionSpec as P

CAP = 12
NZ, NY, NDP = 8, 4, 4
TOK = 64
ALL = NZ * TOK
BLK = NZ * CAP
ROWS = NY * BLK
HALF = 1024
AUX = 128
WIDE = HALF + AUX
G_AT = WIDE
SLICE = 512
QUARTER = SLICE // 2
BF, F32 = jnp.bfloat16, jnp.float32
VMEM_LIMIT = 40 * 1024 * 1024

Z_PERM = {k: [(z * NY + y, (z + k) % NZ * NY + y) for z in range(NZ) for y in range(NY)] for k in (1, -1)}
Y_PERM = {k: [(z * NY + y, z * NY + (y + k) % NY) for z in range(NZ) for y in range(NY)] for k in (1, 2, 3)}
D_PERM = {k: [(i, (i + k) % NDP) for i in range(NDP)] for k in (1, -1)}
T_PERM = [(0, 1), (1, 0)]


def z_shift(v, k):
    return lax.ppermute(v, "expert", Z_PERM[k])


def y_shift(v, k):
    return lax.ppermute(v, "expert", Y_PERM[k])


def d_shift(v, k):
    return lax.ppermute(v, "dp", D_PERM[k])


def swap(v):
    return lax.ppermute(v, "tensor", T_PERM)


def call(kernel, outs, ins, scratch=(), grid=None, in_specs=None, out_specs=None):
    extra = {} if grid is None else {"grid": grid}
    vm = pl.BlockSpec(memory_space=pltpu.VMEM)
    return pl.pallas_call(
        kernel,
        out_shape=outs,
        in_specs=in_specs or [vm] * len(ins),
        out_specs=out_specs or [vm] * len(outs),
        scratch_shapes=list(scratch),
        compiler_params=pltpu.CompilerParams(vmem_limit_bytes=VMEM_LIMIT),
        cost_estimate=pl.CostEstimate(flops=0, bytes_accessed=0, transcendentals=0),
        **extra,
    )(*ins)


def shape(*dims, dtype=BF):
    return jax.ShapeDtypeStruct(dims, dtype)


SMEM = pl.BlockSpec(memory_space=pltpu.SMEM)
VM = pl.BlockSpec(memory_space=pltpu.VMEM)


def place(pieces, into, cols):
    row = 0
    for ref in pieces:
        n = ref.shape[0]
        into[row : row + n, :] = ref[:, cols].astype(into.dtype)
        row += n


def one_hot(tab, oh, weighted):
    slot = lax.broadcasted_iota(jnp.int32, (BLK, ALL), 0).astype(F32)
    for e in range(2 * NY):
        value = tab[8 + e : 9 + e, :] if weighted else 1.0
        oh[e * BLK : (e + 1) * BLK, :] = jnp.where(tab[e : e + 1, :] == slot, value, 0.0).astype(BF)


def pick(oh, full, outs):
    for k, out in enumerate(outs):
        rows = jnp.dot(oh[k * 2 * BLK : (k + 1) * 2 * BLK, :], full[...], preferred_element_type=F32).astype(BF)
        out[0] = rows[:BLK]
        out[1] = rows[BLK:]


def pick_kernel(experts, *refs):
    pieces, x_outs, g_outs, (tab, grads), (full, aux, hits, oh) = refs[:9], refs[9:13], refs[13:17], refs[17:19], refs[19:]
    place(pieces, full, slice(0, HALF))
    place(pieces, aux, slice(HALF, WIDE))
    turned = aux[...].T
    ids = turned[0:8, :].astype(jnp.int32)
    weights = turned[8:16, :]
    tab[16:24, :] = turned[0:8, :]
    hits[...] = jnp.zeros_like(hits)
    for e in range(2 * NY):
        same = ids == experts[e]
        hits[e : e + 1, :] = jnp.sum(jnp.where(same, 1.0, 0.0), axis=0, keepdims=True)
        tab[8 + e : 9 + e, :] = jnp.sum(jnp.where(same, weights, 0.0), axis=0, keepdims=True)
    before = lax.broadcasted_iota(jnp.int32, (ALL, ALL), 0)
    after = lax.broadcasted_iota(jnp.int32, (ALL, ALL), 1)
    earlier = jnp.where((before < after) & (before // TOK == after // TOK), 1.0, 0.0).astype(BF)
    rank = jnp.dot(hits[...].astype(BF), earlier, preferred_element_type=F32)
    block = (lax.broadcasted_iota(jnp.int32, (8, ALL), 1) // TOK).astype(F32)
    tab[0:8, :] = jnp.where(hits[0:8, :] > 0.0, block * CAP + rank[0:8, :], -1.0)
    one_hot(tab, oh, False)
    pick(oh, full, x_outs)
    place(pieces, grads, slice(G_AT, G_AT + HALF))
    one_hot(tab, oh, True)
    pick(oh, grads, g_outs)


def gather_rows(own, other, rows, core):
    for k in range(NY):
        span = slice(k * BLK, (k + 1) * BLK)
        rows[span, pl.ds(pl.multiple_of(core * HALF, HALF), HALF)] = own[k, 0]
        rows[span, pl.ds(pl.multiple_of((1 - core) * HALF, HALF), HALF)] = other[k, 0]


def forward_kernel(info, *refs):
    own, other, w_gate, w_up, w_down, slices, act, slope, hidden, send, rows = refs
    core = info[0]
    gather_rows(own, other, rows, core)
    for k in range(NDP):
        slices[k, 0] = rows[:, pl.ds(pl.multiple_of(k * SLICE + core * QUARTER, QUARTER), QUARTER)]
    gate = jnp.dot(rows[...], w_gate[0], preferred_element_type=F32)
    up = jnp.dot(rows[...], w_up[0], preferred_element_type=F32)
    sig = jax.nn.sigmoid(gate)
    activated = gate * sig
    act[0] = activated
    slope[0] = up * sig * (1.0 + gate * (1.0 - sig))
    hid = (activated * up).astype(BF)
    hidden[0] = hid
    far = w_down[0, :, pl.ds(pl.multiple_of((1 - core) * HALF, HALF), HALF)]
    send[0] = jnp.dot(hid, far, preferred_element_type=F32).astype(BF)


def out_kernel(info, hidden, w_down, got, *outs):
    near = w_down[0, :, pl.ds(pl.multiple_of(info[0] * HALF, HALF), HALF)]
    total = jnp.dot(hidden[0], near, preferred_element_type=F32) + got[0].astype(F32)
    for k in range(NY):
        outs[k][0] = total[k * BLK : (k + 1) * BLK].astype(BF)


NT = (((1,), (1,)), ((), ()))
TN = (((0,), (0,)), ((), ()))


def backward_kernel(info, *refs):
    own, other, w_gate, w_up, w_down, act, slope, hidden, gg, send, down, rows = refs
    core = info[0]
    gather_rows(own, other, rows, core)
    grad = lax.dot_general(rows[...], w_down[0], NT, preferred_element_type=F32)
    d_gate = (grad * slope[0]).astype(BF)
    d_up = (grad * act[0]).astype(BF)
    gg[0, :, 0:384] = d_gate
    gg[0, :, 384:768] = d_up
    far = pl.ds(pl.multiple_of((1 - core) * HALF, HALF), HALF)
    total = lax.dot_general(d_gate, w_gate[0, far, :], NT, preferred_element_type=F32)
    total = total + lax.dot_general(d_up, w_up[0, far, :], NT, preferred_element_type=F32)
    send[0] = total.astype(BF)
    for k in range(NDP):
        part = rows[:, k * SLICE : (k + 1) * SLICE]
        down[k, 0] = lax.dot_general(hidden[0], part, TN, preferred_element_type=F32).astype(BF)


def dx_kernel(info, gg, w_gate, w_up, got, *outs):
    near = pl.ds(pl.multiple_of(info[0] * HALF, HALF), HALF)
    total = lax.dot_general(gg[0, :, 0:384], w_gate[0, near, :], NT, preferred_element_type=F32)
    total = total + lax.dot_general(gg[0, :, 384:768], w_up[0, near, :], NT, preferred_element_type=F32)
    total = total + got[0].astype(F32)
    for k in range(NY):
        outs[k][0] = total[k * BLK : (k + 1) * BLK].astype(BF)


def lay_rows(pieces, rows):
    for k, ref in enumerate(pieces):
        for j in range(2):
            rows[(2 * k + j) * BLK : (2 * k + j + 1) * BLK, :] = ref[j]


def spread(total, outs, cols):
    near, (top, low), far = outs[:4], outs[4:6], outs[6:]
    for d in range(4):
        near[d][:, cols] = total[d * TOK : (d + 1) * TOK]
    top[:, cols] = total[4 * TOK : 4 * TOK + TOK // 2].astype(BF)
    low[:, cols] = total[4 * TOK + TOK // 2 : 5 * TOK].astype(BF)
    for d in range(3):
        far[d][:, cols] = total[(5 + d) * TOK : (6 + d) * TOK]


def mix_kernel(experts, tab, grads, *refs):
    pieces, out, (rows, oh, turned) = refs[:4], refs[4], refs[5:]
    lay_rows(pieces, rows)
    one_hot(tab, oh, True)
    out[:, 0:HALF] = lax.dot_general(oh[...], rows[...], TN, preferred_element_type=F32)
    scores = lax.dot_general(rows[...], grads[...], NT, preferred_element_type=F32)
    slot = lax.broadcasted_iota(jnp.int32, (BLK, ALL), 0).astype(F32)
    ids = tab[16:24, :].astype(jnp.int32)
    found = jnp.zeros((8, ALL), F32)
    for e in range(2 * NY):
        mine = jnp.where(tab[e : e + 1, :] == slot, scores[e * BLK : (e + 1) * BLK, :], 0.0)
        mine = jnp.sum(mine, axis=0, keepdims=True)
        found = found + jnp.where(ids == experts[e], mine, 0.0)
    high = found.astype(BF).astype(F32)
    turned[...] = jnp.zeros_like(turned)
    turned[0:8, :] = high
    turned[8:16, :] = found - high
    out[:, HALF:WIDE] = turned[...].T


def unpick_kernel(tab, *refs):
    pieces, mixed, outs, (rows, oh) = refs[:4], refs[4], refs[5:14], refs[14:]
    lay_rows(pieces, rows)
    one_hot(tab, oh, False)
    total = lax.dot_general(oh[...], rows[...], TN, preferred_element_type=F32)
    spread(mixed, outs, slice(0, WIDE))
    spread(total, outs, slice(WIDE, WIDE + HALF))


def gate_up_kernel(info, near, far, g0, g1, g2a, g2b, g3, d_gate, d_up, rows, grads):
    core = info[0]
    for k in range(NDP):
        span = slice(k * ROWS, (k + 1) * ROWS)
        at = info[1 + k]
        rows[span, pl.ds(pl.multiple_of(core * QUARTER, QUARTER), QUARTER)] = near[at, 0]
        rows[span, pl.ds(pl.multiple_of((1 - core) * QUARTER, QUARTER), QUARTER)] = far[at, 0]
    grads[0:ROWS, :] = g0[0]
    grads[ROWS : 2 * ROWS, :] = g1[0]
    first = pl.program_id(0) == 0
    grads[2 * ROWS : 3 * ROWS, :] = jnp.where(first, g2a[...], g2b[...])
    grads[3 * ROWS : 4 * ROWS, :] = g3[0]
    total = lax.dot_general(rows[...], grads[...], TN, preferred_element_type=F32)
    d_gate[0] = total[:, 0:384].astype(BF)
    d_up[0] = total[:, 384:768].astype(BF)


def after(value, *earlier):
    return lax.optimization_barrier((value, earlier))[0]


def z_gather(v):
    h = TOK // 2
    r1, l1 = z_shift(v, 1), z_shift(v, -1)
    r2, l2 = z_shift(r1, 1), z_shift(l1, -1)
    r3, l3 = z_shift(r2, 1), z_shift(l2, -1)
    r4, l4 = z_shift(r3[:h], 1), z_shift(l3[h:], -1)
    return [v, r1, r2, r3, r4, l4, l3, l2, l1]


def z_begin(p3, top, low, p5, p2, p6):
    h = TOK // 2
    r, l = z_shift(top, 1).astype(F32), z_shift(low, -1).astype(F32)
    r = p5 + jnp.pad(r, ((0, h), (0, 0)))
    l = p3 + jnp.pad(l, ((h, 0), (0, 0)))
    return z_step(r, l, p6, p2)


def z_step(r, l, right, left):
    return right + z_shift(r.astype(BF), 1).astype(F32), left + z_shift(l.astype(BF), -1).astype(F32)


def of_expert(*dims):
    return pl.BlockSpec((1,) + dims, lambda e: (e,) + (0,) * len(dims))


def per_device(tokens, expert_ids, route_weights, grad_out, w_gate, w_up, w_down):
    core = lax.axis_index("tensor")
    at = lax.axis_index("expert")
    z, y = at // NY, at % NY
    owners = (y + jnp.arange(2 * NY, dtype=jnp.int32) // 2) % NY
    experts = z * 2 * NY + owners * 2 + jnp.arange(2 * NY, dtype=jnp.int32) % 2
    dp = lax.axis_index("dp")
    info = jnp.concatenate([core[None], (dp + NDP - jnp.arange(NDP, dtype=jnp.int32)) % NDP]).astype(jnp.int32)

    x_half = lax.dynamic_slice_in_dim(tokens, core * HALF, HALF, axis=1)
    g_half = lax.dynamic_slice_in_dim(grad_out, core * HALF, HALF, axis=1)
    aux = jnp.concatenate([expert_ids.astype(BF), route_weights, jnp.zeros((TOK, AUX - 16), BF)], axis=1)
    pieces = z_gather(jnp.concatenate([x_half, aux, g_half], axis=1))

    ring = [shape(2, BLK, HALF)] * NY
    *rows, tab, grads = call(
        pick_kernel,
        ring * 2 + [shape(24, ALL, dtype=F32), shape(ALL, HALF)],
        [experts] + pieces,
        [pltpu.VMEM((ALL, HALF), BF), pltpu.VMEM((ALL, AUX), F32), pltpu.VMEM((16, ALL), F32), pltpu.VMEM((2 * ROWS, ALL), BF)],
        in_specs=[SMEM] + [VM] * 9,
    )
    x_rows, g_rows = rows[:NY], rows[NY:]
    x_own = [x_rows[0]] + [y_shift(x_rows[k], k) for k in (1, 2, 3)]
    x_own = jnp.stack(x_own)
    x_far = swap(x_own)
    g_rows = after(g_rows, x_own)
    g_own = [g_rows[0]] + [y_shift(g_rows[k], k) for k in (1, 2, 3)]

    block = [of_expert(BLK, HALF)] * 4
    wg_spec, wd_spec = of_expert(2048, 384), of_expert(384, 2048)
    sq, half_spec, row_spec = of_expert(ROWS, 384), of_expert(ROWS, HALF), of_expert(ROWS, 2048)
    far_spec = pl.BlockSpec((NY, 1, BLK, HALF), lambda e: (0, e, 0, 0))
    cut = pl.BlockSpec((NDP, 1, ROWS, QUARTER), lambda e: (0, e, 0, 0))
    x_slices, act, slope, hidden, out_send = call(
        forward_kernel,
        [shape(NDP, 2, ROWS, QUARTER)] + [shape(2, ROWS, 384, dtype=F32)] * 2 + [shape(2, ROWS, 384), shape(2, ROWS, HALF)],
        [info, x_own, x_far, w_gate, w_up, w_down],
        [pltpu.VMEM((ROWS, 2048), BF)],
        grid=(2,),
        in_specs=[SMEM, far_spec, far_spec, wg_spec, wg_spec, wd_spec],
        out_specs=[cut, sq, sq, sq, half_spec],
    )
    g_own, x_slices, out_send, hidden = lax.optimization_barrier((g_own, x_slices, out_send, hidden))
    x_near = lax.all_to_all(x_slices, "dp", split_axis=0, concat_axis=0, tiled=True)
    out_got = swap(out_send)
    g_own = jnp.stack(g_own)
    g_far = swap(g_own)
    gg, dx_send, down_part = call(
        backward_kernel,
        [shape(2, ROWS, 768), shape(2, ROWS, HALF), shape(NDP, 2, 384, SLICE)],
        [info, g_own, g_far, w_gate, w_up, w_down, act, slope, hidden],
        [pltpu.VMEM((ROWS, 2048), BF)],
        grid=(2,),
        in_specs=[SMEM, far_spec, far_spec, wg_spec, wg_spec, wd_spec, sq, sq, sq],
        out_specs=[of_expert(ROWS, 768), half_spec, pl.BlockSpec((NDP, 1, 384, SLICE), lambda e: (0, e, 0, 0))],
    )
    grad_down = lax.psum_scatter(down_part, "dp", scatter_dimension=0, tiled=True)
    gg, dx_send, out_got = lax.optimization_barrier((gg, dx_send, out_got))
    out_rows = call(
        out_kernel,
        ring,
        [info, hidden, w_down, out_got],
        grid=(2,),
        in_specs=[SMEM, sq, wd_spec, half_spec],
        out_specs=block,
    )
    out_back = [out_rows[0]] + [y_shift(out_rows[k], NY - k) for k in (1, 2, 3)]
    dx_got, x_near = lax.optimization_barrier((swap(dx_send), x_near))
    dx_rows = call(
        dx_kernel,
        ring,
        [info, gg, w_gate, w_up, dx_got],
        grid=(2,),
        in_specs=[SMEM, of_expert(ROWS, 768), wg_spec, wg_spec, half_spec],
        out_specs=block,
    )

    def parts(width):
        full, split = shape(TOK, width, dtype=F32), shape(TOK // 2, width)
        return [full] * 4 + [split] * 2 + [full] * 3

    dx_back = [dx_rows[0]] + [y_shift(dx_rows[k], NY - k) for k in (1, 2, 3)]
    (mixed_parts,) = call(
        mix_kernel,
        [shape(ALL, WIDE, dtype=F32)],
        [experts, tab, grads] + out_back,
        [pltpu.VMEM((2 * ROWS, HALF), BF), pltpu.VMEM((2 * ROWS, ALL), BF), pltpu.VMEM((AUX, ALL), F32)],
        in_specs=[SMEM] + [VM] * 6,
    )
    right, left = d_shift(gg, 1), d_shift(gg, -1)
    dx_back, mixed_parts, right, left, x_near = lax.optimization_barrier((dx_back, mixed_parts, right, left, x_near))
    x_got = swap(x_near)
    p0, p1, p2, p3, top, low, p5, p6, p7 = call(
        unpick_kernel,
        parts(WIDE + HALF),
        [tab] + dx_back + [mixed_parts],
        [pltpu.VMEM((2 * ROWS, HALF), BF), pltpu.VMEM((2 * ROWS, ALL), BF)],
    )
    gg_all = [gg, right, d_shift(right[0], 1), d_shift(left[1], -1), left]
    r, l = z_begin(p3, top, low, p5, p2, p6)
    r, l, gg_all, x_got = lax.optimization_barrier((r, l, gg_all, x_got))
    r, l = z_step(r, l, p7, p1)
    gg_spec, whole = of_expert(ROWS, 768), pl.BlockSpec((ROWS, 768), lambda e: (0, 0))
    grad_gate, grad_up = call(
        gate_up_kernel,
        [shape(2, SLICE, 384)] * 2,
        [info, x_near, x_got] + gg_all,
        [pltpu.VMEM((NDP * ROWS, SLICE), BF), pltpu.VMEM((NDP * ROWS, 768), BF)],
        grid=(2,),
        in_specs=[SMEM, cut, cut, gg_spec, gg_spec, whole, whole, gg_spec],
        out_specs=[of_expert(SLICE, 384)] * 2,
    )
    r, l, grad_gate, grad_up = lax.optimization_barrier((r, l, grad_gate, grad_up))
    half = p0 + z_shift(r.astype(BF), 1).astype(F32) + z_shift(l.astype(BF), -1).astype(F32)
    mixed_half, dx_half = half[:, :WIDE], half[:, WIDE:].astype(BF)

    def both(half):
        other = swap(half)
        low, high = jnp.where(core == 0, half, other), jnp.where(core == 0, other, half)
        return jnp.concatenate([low, high], axis=1)

    mixed = both(mixed_half[:, :HALF].astype(BF))
    weight_half = mixed_half[:, HALF : HALF + 8] + mixed_half[:, HALF + 8 : HALF + 16]
    grad_weights = weight_half + swap(weight_half)
    grad_x = both(dx_half)
    grad_down = grad_down.reshape(2, 384, SLICE)
    return mixed, grad_x, grad_weights, grad_gate, grad_up, grad_down


def solution(mesh):
    tok = P(("dp", "expert"), None)
    return jax.shard_map(
        per_device,
        mesh=mesh,
        in_specs=(tok, tok, tok, tok, P("expert", None, "tensor"), P("expert", None, "tensor"), P("expert", "tensor", None)),
        out_specs=(tok, tok, tok, P("expert", "dp", "tensor"), P("expert", "dp", "tensor"), P("expert", "tensor", "dp")),
        check_vma=False,
    )
```

```python
import jax
import jax.numpy as jnp
from jax import lax
from jax.experimental import pallas as pl
from jax.experimental.pallas import tpu as pltpu
from jax.sharding import PartitionSpec as P

CAP = 12
NZ, NY, NDP = 8, 4, 4
TOK = 64
ALL = NZ * TOK
BLK = NZ * CAP
ROWS = NY * BLK
HALF = 1024
AUX = 128
WIDE = HALF + AUX
G_AT = WIDE
SLICE = 512
QUARTER = SLICE // 2
BF, F32 = jnp.bfloat16, jnp.float32
VMEM_LIMIT = 50 * 1024 * 1024

Z_PERM = {k: [(z * NY + y, (z + k) % NZ * NY + y) for z in range(NZ) for y in range(NY)] for k in (1, -1)}
Y_PERM = {k: [(z * NY + y, z * NY + (y + k) % NY) for z in range(NZ) for y in range(NY)] for k in (1, 2, 3)}
D_PERM = {k: [(i, (i + k) % NDP) for i in range(NDP)] for k in (1, -1)}
T_PERM = [(0, 1), (1, 0)]


def z_shift(v, k):
    return lax.ppermute(v, "expert", Z_PERM[k])


def y_shift(v, k):
    return lax.ppermute(v, "expert", Y_PERM[k])


def d_shift(v, k):
    return lax.ppermute(v, "dp", D_PERM[k])


def swap(v):
    return lax.ppermute(v, "tensor", T_PERM)


def call(kernel, outs, ins, scratch=(), grid=None, in_specs=None, out_specs=None):
    extra = {} if grid is None else {"grid": grid}
    vm = pl.BlockSpec(memory_space=pltpu.VMEM)
    return pl.pallas_call(
        kernel,
        out_shape=outs,
        in_specs=in_specs or [vm] * len(ins),
        out_specs=out_specs or [vm] * len(outs),
        scratch_shapes=list(scratch),
        compiler_params=pltpu.CompilerParams(vmem_limit_bytes=VMEM_LIMIT),
        cost_estimate=pl.CostEstimate(flops=0, bytes_accessed=0, transcendentals=0),
        **extra,
    )(*ins)


def shape(*dims, dtype=BF):
    return jax.ShapeDtypeStruct(dims, dtype)


SMEM = pl.BlockSpec(memory_space=pltpu.SMEM)
VM = pl.BlockSpec(memory_space=pltpu.VMEM)


def place(pieces, into, cols):
    row = 0
    for ref in pieces:
        n = ref.shape[0]
        into[row : row + n, :] = ref[:, cols].astype(into.dtype)
        row += n


def one_hot(tab, oh, weighted):
    slot = lax.broadcasted_iota(jnp.int32, (BLK, ALL), 0).astype(F32)
    for e in range(2 * NY):
        value = tab[8 + e : 9 + e, :] if weighted else 1.0
        oh[e * BLK : (e + 1) * BLK, :] = jnp.where(tab[e : e + 1, :] == slot, value, 0.0).astype(BF)


def pick(oh, full, outs):
    for k, out in enumerate(outs):
        rows = jnp.dot(oh[k * 2 * BLK : (k + 1) * 2 * BLK, :], full[...], preferred_element_type=F32).astype(BF)
        out[0] = rows[:BLK]
        out[1] = rows[BLK:]


def pick_kernel(experts, *refs):
    pieces, x_outs, g_outs, (tab, grads), (full, aux, hits, oh) = refs[:9], refs[9:13], refs[13:17], refs[17:19], refs[19:]
    place(pieces, full, slice(0, HALF))
    place(pieces, aux, slice(HALF, WIDE))
    turned = aux[...].T
    ids = turned[0:8, :].astype(jnp.int32)
    weights = turned[8:16, :]
    tab[16:24, :] = turned[0:8, :]
    hits[...] = jnp.zeros_like(hits)
    for e in range(2 * NY):
        same = ids == experts[e]
        hits[e : e + 1, :] = jnp.sum(jnp.where(same, 1.0, 0.0), axis=0, keepdims=True)
        tab[8 + e : 9 + e, :] = jnp.sum(jnp.where(same, weights, 0.0), axis=0, keepdims=True)
    before = lax.broadcasted_iota(jnp.int32, (ALL, ALL), 0)
    after = lax.broadcasted_iota(jnp.int32, (ALL, ALL), 1)
    earlier = jnp.where((before < after) & (before // TOK == after // TOK), 1.0, 0.0).astype(BF)
    rank = jnp.dot(hits[...].astype(BF), earlier, preferred_element_type=F32)
    block = (lax.broadcasted_iota(jnp.int32, (8, ALL), 1) // TOK).astype(F32)
    tab[0:8, :] = jnp.where(hits[0:8, :] > 0.0, block * CAP + rank[0:8, :], -1.0)
    one_hot(tab, oh, False)
    pick(oh, full, x_outs)
    place(pieces, grads, slice(G_AT, G_AT + HALF))
    one_hot(tab, oh, True)
    pick(oh, grads, g_outs)


def gather_rows(own, other, rows, core):
    for k in range(NY):
        span = slice(k * BLK, (k + 1) * BLK)
        rows[span, pl.ds(pl.multiple_of(core * HALF, HALF), HALF)] = own[k, 0]
        rows[span, pl.ds(pl.multiple_of((1 - core) * HALF, HALF), HALF)] = other[k, 0]


def forward_kernel(info, *refs):
    own, other, w_gate, w_up, w_down, slices, act, slope, hidden, send, rows = refs
    core = info[0]
    gather_rows(own, other, rows, core)
    for k in range(NDP):
        slices[k, 0] = rows[:, pl.ds(pl.multiple_of(k * SLICE + core * QUARTER, QUARTER), QUARTER)]
    gate = jnp.dot(rows[...], w_gate[0], preferred_element_type=F32)
    up = jnp.dot(rows[...], w_up[0], preferred_element_type=F32)
    sig = jax.nn.sigmoid(gate)
    activated = gate * sig
    act[0] = activated
    slope[0] = up * sig * (1.0 + gate * (1.0 - sig))
    hid = (activated * up).astype(BF)
    hidden[0] = hid
    far = w_down[0, :, pl.ds(pl.multiple_of((1 - core) * HALF, HALF), HALF)]
    send[0] = jnp.dot(hid, far, preferred_element_type=F32).astype(BF)


def out_kernel(info, hidden, w_down, got, *outs):
    near = w_down[0, :, pl.ds(pl.multiple_of(info[0] * HALF, HALF), HALF)]
    total = jnp.dot(hidden[0], near, preferred_element_type=F32) + got[0].astype(F32)
    for k in range(NY):
        outs[k][0] = total[k * BLK : (k + 1) * BLK].astype(BF)


NT = (((1,), (1,)), ((), ()))
TN = (((0,), (0,)), ((), ()))


def backward_kernel(info, *refs):
    own, other, w_gate, w_up, w_down, act, slope, hidden, gg, send, down, rows = refs
    core = info[0]
    gather_rows(own, other, rows, core)
    grad = lax.dot_general(rows[...], w_down[0], NT, preferred_element_type=F32)
    d_gate = (grad * slope[0]).astype(BF)
    d_up = (grad * act[0]).astype(BF)
    gg[0, :, 0:384] = d_gate
    gg[0, :, 384:768] = d_up
    far = pl.ds(pl.multiple_of((1 - core) * HALF, HALF), HALF)
    total = lax.dot_general(d_gate, w_gate[0, far, :], NT, preferred_element_type=F32)
    total = total + lax.dot_general(d_up, w_up[0, far, :], NT, preferred_element_type=F32)
    send[0] = total.astype(BF)
    for k in range(NDP):
        part = rows[:, k * SLICE : (k + 1) * SLICE]
        down[k, 0] = lax.dot_general(hidden[0], part, TN, preferred_element_type=F32).astype(BF)


def dx_kernel(info, gg, w_gate, w_up, got, *outs):
    near = pl.ds(pl.multiple_of(info[0] * HALF, HALF), HALF)
    total = lax.dot_general(gg[0, :, 0:384], w_gate[0, near, :], NT, preferred_element_type=F32)
    total = total + lax.dot_general(gg[0, :, 384:768], w_up[0, near, :], NT, preferred_element_type=F32)
    total = total + got[0].astype(F32)
    for k in range(NY):
        outs[k][0] = total[k * BLK : (k + 1) * BLK].astype(BF)


def lay_rows(pieces, rows):
    for k, ref in enumerate(pieces):
        for j in range(2):
            rows[(2 * k + j) * BLK : (2 * k + j + 1) * BLK, :] = ref[j]


def spread(total, outs, cols):
    near, (top, low), far = outs[:4], outs[4:6], outs[6:]
    for d in range(4):
        near[d][:, cols] = total[d * TOK : (d + 1) * TOK]
    top[:, cols] = total[4 * TOK : 4 * TOK + TOK // 2].astype(BF)
    low[:, cols] = total[4 * TOK + TOK // 2 : 5 * TOK].astype(BF)
    for d in range(3):
        far[d][:, cols] = total[(5 + d) * TOK : (6 + d) * TOK]


def mix_kernel(experts, tab, grads, *refs):
    pieces, out, (rows, oh, turned) = refs[:4], refs[4], refs[5:]
    lay_rows(pieces, rows)
    one_hot(tab, oh, True)
    out[:, 0:HALF] = lax.dot_general(oh[...], rows[...], TN, preferred_element_type=F32)
    scores = lax.dot_general(rows[...], grads[...], NT, preferred_element_type=F32)
    slot = lax.broadcasted_iota(jnp.int32, (BLK, ALL), 0).astype(F32)
    ids = tab[16:24, :].astype(jnp.int32)
    found = jnp.zeros((8, ALL), F32)
    for e in range(2 * NY):
        mine = jnp.where(tab[e : e + 1, :] == slot, scores[e * BLK : (e + 1) * BLK, :], 0.0)
        mine = jnp.sum(mine, axis=0, keepdims=True)
        found = found + jnp.where(ids == experts[e], mine, 0.0)
    high = found.astype(BF).astype(F32)
    turned[...] = jnp.zeros_like(turned)
    turned[0:8, :] = high
    turned[8:16, :] = found - high
    out[:, HALF:WIDE] = turned[...].T


def unpick_kernel(tab, *refs):
    pieces, mixed, outs, (rows, oh) = refs[:4], refs[4], refs[5:14], refs[14:]
    lay_rows(pieces, rows)
    one_hot(tab, oh, False)
    total = lax.dot_general(oh[...], rows[...], TN, preferred_element_type=F32)
    spread(mixed, outs, slice(0, WIDE))
    spread(total, outs, slice(WIDE, WIDE + HALF))


def gate_up_kernel(info, near, far, g0, g1, g2a, g2b, g3, d_gate, d_up, rows, grads):
    core = info[0]
    for k in range(NDP):
        span = slice(k * ROWS, (k + 1) * ROWS)
        at = info[1 + k]
        rows[span, pl.ds(pl.multiple_of(core * QUARTER, QUARTER), QUARTER)] = near[at, 0]
        rows[span, pl.ds(pl.multiple_of((1 - core) * QUARTER, QUARTER), QUARTER)] = far[at, 0]
    grads[0:ROWS, :] = g0[0]
    grads[ROWS : 2 * ROWS, :] = g1[0]
    first = pl.program_id(0) == 0
    grads[2 * ROWS : 3 * ROWS, :] = jnp.where(first, g2a[...], g2b[...])
    grads[3 * ROWS : 4 * ROWS, :] = g3[0]
    total = lax.dot_general(rows[...], grads[...], TN, preferred_element_type=F32)
    d_gate[0] = total[:, 0:384].astype(BF)
    d_up[0] = total[:, 384:768].astype(BF)


def after(value, *earlier):
    return lax.optimization_barrier((value, earlier))[0]


def z_gather(v):
    h = TOK // 2
    r1, l1 = z_shift(v, 1), z_shift(v, -1)
    r2, l2 = z_shift(r1, 1), z_shift(l1, -1)
    r3, l3 = z_shift(r2, 1), z_shift(l2, -1)
    r4, l4 = z_shift(r3[:h], 1), z_shift(l3[h:], -1)
    return [v, r1, r2, r3, r4, l4, l3, l2, l1]


def z_begin(p3, top, low, p5, p2, p6):
    h = TOK // 2
    r, l = z_shift(top, 1).astype(F32), z_shift(low, -1).astype(F32)
    r = p5 + jnp.pad(r, ((0, h), (0, 0)))
    l = p3 + jnp.pad(l, ((h, 0), (0, 0)))
    return z_step(r, l, p6, p2)


def z_step(r, l, right, left):
    return right + z_shift(r.astype(BF), 1).astype(F32), left + z_shift(l.astype(BF), -1).astype(F32)


def of_expert(*dims):
    return pl.BlockSpec((1,) + dims, lambda e: (e,) + (0,) * len(dims))


def per_device(tokens, expert_ids, route_weights, grad_out, w_gate, w_up, w_down):
    core = lax.axis_index("tensor")
    at = lax.axis_index("expert")
    z, y = at // NY, at % NY
    owners = (y + jnp.arange(2 * NY, dtype=jnp.int32) // 2) % NY
    experts = z * 2 * NY + owners * 2 + jnp.arange(2 * NY, dtype=jnp.int32) % 2
    dp = lax.axis_index("dp")
    info = jnp.concatenate([core[None], (dp + NDP - jnp.arange(NDP, dtype=jnp.int32)) % NDP]).astype(jnp.int32)

    x_half = lax.dynamic_slice_in_dim(tokens, core * HALF, HALF, axis=1)
    g_half = lax.dynamic_slice_in_dim(grad_out, core * HALF, HALF, axis=1)
    aux = jnp.concatenate([expert_ids.astype(BF), route_weights, jnp.zeros((TOK, AUX - 16), BF)], axis=1)
    pieces = z_gather(jnp.concatenate([x_half, aux, g_half], axis=1))

    ring = [shape(2, BLK, HALF)] * NY
    *rows, tab, grads = call(
        pick_kernel,
        ring * 2 + [shape(24, ALL, dtype=F32), shape(ALL, HALF)],
        [experts] + pieces,
        [pltpu.VMEM((ALL, HALF), BF), pltpu.VMEM((ALL, AUX), F32), pltpu.VMEM((16, ALL), F32), pltpu.VMEM((2 * ROWS, ALL), BF)],
        in_specs=[SMEM] + [VM] * 9,
    )
    x_rows, g_rows = rows[:NY], rows[NY:]
    x_own = [x_rows[0]] + [y_shift(x_rows[k], k) for k in (1, 2, 3)]
    x_own = jnp.stack(x_own)
    x_far = swap(x_own)
    g_rows = after(g_rows, x_own)
    g_own = [g_rows[0]] + [y_shift(g_rows[k], k) for k in (1, 2, 3)]

    block = [of_expert(BLK, HALF)] * 4
    wg_spec, wd_spec = of_expert(2048, 384), of_expert(384, 2048)
    sq, half_spec, row_spec = of_expert(ROWS, 384), of_expert(ROWS, HALF), of_expert(ROWS, 2048)
    far_spec = pl.BlockSpec((NY, 1, BLK, HALF), lambda e: (0, e, 0, 0))
    cut = pl.BlockSpec((NDP, 1, ROWS, QUARTER), lambda e: (0, e, 0, 0))
    x_slices, act, slope, hidden, out_send = call(
        forward_kernel,
        [shape(NDP, 2, ROWS, QUARTER)] + [shape(2, ROWS, 384, dtype=F32)] * 2 + [shape(2, ROWS, 384), shape(2, ROWS, HALF)],
        [info, x_own, x_far, w_gate, w_up, w_down],
        [pltpu.VMEM((ROWS, 2048), BF)],
        grid=(2,),
        in_specs=[SMEM, far_spec, far_spec, wg_spec, wg_spec, wd_spec],
        out_specs=[cut, sq, sq, sq, half_spec],
    )
    g_own, x_slices, out_send, hidden = lax.optimization_barrier((g_own, x_slices, out_send, hidden))
    x_near = lax.all_to_all(x_slices, "dp", split_axis=0, concat_axis=0, tiled=True)
    out_got = swap(out_send)
    g_own = jnp.stack(g_own)
    g_far = swap(g_own)
    gg, dx_send, down_part = call(
        backward_kernel,
        [shape(2, ROWS, 768), shape(2, ROWS, HALF), shape(NDP, 2, 384, SLICE)],
        [info, g_own, g_far, w_gate, w_up, w_down, act, slope, hidden],
        [pltpu.VMEM((ROWS, 2048), BF)],
        grid=(2,),
        in_specs=[SMEM, far_spec, far_spec, wg_spec, wg_spec, wd_spec, sq, sq, sq],
        out_specs=[of_expert(ROWS, 768), half_spec, pl.BlockSpec((NDP, 1, 384, SLICE), lambda e: (0, e, 0, 0))],
    )
    grad_down = lax.psum_scatter(down_part, "dp", scatter_dimension=0, tiled=True)
    gg, dx_send, out_got = lax.optimization_barrier((gg, dx_send, out_got))
    out_rows = call(
        out_kernel,
        ring,
        [info, hidden, w_down, out_got],
        grid=(2,),
        in_specs=[SMEM, sq, wd_spec, half_spec],
        out_specs=block,
    )
    out_back = [out_rows[0]] + [y_shift(out_rows[k], NY - k) for k in (1, 2, 3)]
    dx_got, x_near = lax.optimization_barrier((swap(dx_send), x_near))
    dx_rows = call(
        dx_kernel,
        ring,
        [info, gg, w_gate, w_up, dx_got],
        grid=(2,),
        in_specs=[SMEM, of_expert(ROWS, 768), wg_spec, wg_spec, half_spec],
        out_specs=block,
    )

    def parts(width):
        full, split = shape(TOK, width, dtype=F32), shape(TOK // 2, width)
        return [full] * 4 + [split] * 2 + [full] * 3

    dx_back = [dx_rows[0]] + [y_shift(dx_rows[k], NY - k) for k in (1, 2, 3)]
    (mixed_parts,) = call(
        mix_kernel,
        [shape(ALL, WIDE, dtype=F32)],
        [experts, tab, grads] + out_back,
        [pltpu.VMEM((2 * ROWS, HALF), BF), pltpu.VMEM((2 * ROWS, ALL), BF), pltpu.VMEM((AUX, ALL), F32)],
        in_specs=[SMEM] + [VM] * 6,
    )
    right, left = d_shift(gg, 1), d_shift(gg, -1)
    dx_back, mixed_parts, right, left, x_near = lax.optimization_barrier((dx_back, mixed_parts, right, left, x_near))
    x_got = swap(x_near)
    p0, p1, p2, p3, top, low, p5, p6, p7 = call(
        unpick_kernel,
        parts(WIDE + HALF),
        [tab] + dx_back + [mixed_parts],
        [pltpu.VMEM((2 * ROWS, HALF), BF), pltpu.VMEM((2 * ROWS, ALL), BF)],
    )
    gg_all = [gg, right, d_shift(right[0], 1), d_shift(left[1], -1), left]
    r, l = z_begin(p3, top, low, p5, p2, p6)
    r, l, gg_all, x_got = lax.optimization_barrier((r, l, gg_all, x_got))
    r, l = z_step(r, l, p7, p1)
    gg_spec, whole = of_expert(ROWS, 768), pl.BlockSpec((ROWS, 768), lambda e: (0, 0))
    grad_gate, grad_up = call(
        gate_up_kernel,
        [shape(2, SLICE, 384)] * 2,
        [info, x_near, x_got] + gg_all,
        [pltpu.VMEM((NDP * ROWS, SLICE), BF), pltpu.VMEM((NDP * ROWS, 768), BF)],
        grid=(2,),
        in_specs=[SMEM, cut, cut, gg_spec, gg_spec, whole, whole, gg_spec],
        out_specs=[of_expert(SLICE, 384)] * 2,
    )
    r, l, grad_gate, grad_up = lax.optimization_barrier((r, l, grad_gate, grad_up))
    half = p0 + z_shift(r.astype(BF), 1).astype(F32) + z_shift(l.astype(BF), -1).astype(F32)
    mixed_half, dx_half = half[:, :WIDE], half[:, WIDE:].astype(BF)

    def both(half):
        other = swap(half)
        low, high = jnp.where(core == 0, half, other), jnp.where(core == 0, other, half)
        return jnp.concatenate([low, high], axis=1)

    mixed = both(mixed_half[:, :HALF].astype(BF))
    weight_half = mixed_half[:, HALF : HALF + 8] + mixed_half[:, HALF + 8 : HALF + 16]
    grad_weights = weight_half + swap(weight_half)
    grad_x = both(dx_half)
    grad_down = grad_down.reshape(2, 384, SLICE)
    return mixed, grad_x, grad_weights, grad_gate, grad_up, grad_down


def solution(mesh):
    tok = P(("dp", "expert"), None)
    return jax.shard_map(
        per_device,
        mesh=mesh,
        in_specs=(tok, tok, tok, tok, P("expert", None, "tensor"), P("expert", None, "tensor"), P("expert", "tensor", None)),
        out_specs=(tok, tok, tok, P("expert", "dp", "tensor"), P("expert", "dp", "tensor"), P("expert", "tensor", "dp")),
        check_vma=False,
    )
```
